32 devices in a mesh: tok: 4 (over y, core), feat: 8 (over z, x).
Axes of the slice: x: 2, y: 2, z: 4, core: 2. Of those that a mesh axis runs over, the one named last changes fastest.
Arguments:
- span_input: bfloat16 [768, 16384], P('tok', 'feat'), may hold values from -6 to 6
- span_output: bfloat16 [768, 16384], P('tok', 'feat'), may hold values from -6 to 6
- block_pairs: int32 [384, 2], replicated, may hold values from 0 to 127, as said below
Outputs:
- gram: float32 [384, 128, 128], P(('tok', 'feat'))
- cross: float32 [384, 128, 128], P(('tok', 'feat'))
The draws below stay inside these ranges and needn't reach their ends.
Inputs may be any that keep to these rules, and one draw needn't show every extreme that they name: `block_pairs`: the pairs are distinct; each of the 128 row blocks appears in exactly 3 pairs, one of them with itself as column block.
All inputs are finite; a program needn't handle non-finite values.
Results may differ from the reference program's by a relative error of at most 0.0003.
Values may be sent and summed in bfloat16 or wider, within the bound.
No kernel may reach another device: no remote copies, remote signals or barrier semaphores. Data moves between devices by JAX's collectives and lax.ppermute only.
A program may use at most 128 MiB of HBM per device.

```python
import jax
import jax.numpy as jnp
from jax import lax

D = 16384
BLK = 128
NB = 128
TOKENS = 768
PAIRS = 384


def draw_block_pairs(key, part):
    per_row = PAIRS // NB
    first_key, second_key = jax.random.split(key)
    scores = jax.random.randint(first_key, (NB, NB - 1), 0, 2 ** 20)
    ranking = jnp.argsort(scores * NB + jnp.arange(NB - 1)[None, :], axis=1).astype(jnp.int32)
    offsets = jnp.concatenate([jnp.zeros((NB, 1), jnp.int32), ranking[:, :per_row - 1] + 1], axis=1)
    row_ids = jnp.broadcast_to(jnp.arange(NB, dtype=jnp.int32)[:, None], (NB, per_row))
    col_ids = (row_ids + offsets) % NB
    listed = jnp.stack([row_ids.reshape(-1), col_ids.reshape(-1)], 1)
    shuffle = jax.random.permutation(second_key, PAIRS)
    return listed[shuffle].astype(jnp.int32)


def levels(rng, shape, pieces, low, largest):
    def one(dim, shards_of):
        steps = jax.random.uniform(jax.random.fold_in(jax.random.fold_in(rng, 6), dim), (shards_of,), jnp.float32, low / len(pieces), largest / len(pieces))
        return jnp.repeat(jnp.exp(steps), shape[dim] // shards_of).reshape((-1,) + (1,) * (len(shape) - dim - 1))

    factor_of = one(*pieces[0])
    for cut in pieces[1:]:
        factor_of = factor_of * one(*cut)
    return factor_of


def normal_values(own_key, shape, deviation, limit, shards=(), held_as=jnp.bfloat16):
    loudness = levels(own_key, shape, shards, -0.22, 0.18) if shards else 1.0
    array = jax.random.normal(own_key, shape, jnp.float32) * deviation * loudness
    return jnp.minimum(jnp.maximum(array, -limit), limit).astype(held_as)


def setup_inputs(seed: int = 0) -> dict:
    key_list = jax.random.split(jax.random.key(seed), 4)
    span_input = normal_values(key_list[0], (TOKENS, D), 1.0, 6.0, ((0, 4), (1, 8)))
    span_output = normal_values(key_list[1], (TOKENS, D), 1.0, 6.0, ((0, 4), (1, 8)))
    block_pairs = draw_block_pairs(jax.random.fold_in(key_list[3], 71), 0)
    return dict(span_input=span_input, span_output=span_output, block_pairs=block_pairs)


def reference(span_input, span_output, block_pairs):
    tok_rows = span_input.shape[0]
    blocks_in = span_input.reshape(tok_rows, NB, BLK)
    blocks_out = span_output.reshape(tok_rows, NB, BLK)

    def pair_stats(listed_pair):
        left_tiles = lax.dynamic_index_in_dim(blocks_in, listed_pair[0], 1, keepdims=False)
        right_in = lax.dynamic_index_in_dim(blocks_in, listed_pair[1], 1, keepdims=False)
        right_out = lax.dynamic_index_in_dim(blocks_out, listed_pair[1], 1, keepdims=False)
        gram_tile = jnp.dot(left_tiles.T, right_in, preferred_element_type=jnp.float32) * (1.0 / TOKENS)
        cross_tile = jnp.dot(left_tiles.T, right_out, preferred_element_type=jnp.float32) * (1.0 / TOKENS)
        return gram_tile, cross_tile

    gram, cross = lax.map(pair_stats, block_pairs)
    return gram, cross
```

```python
import functools

import jax
import jax.numpy as jnp
from jax import lax
from jax.experimental import pallas as pl
from jax.experimental.pallas import tpu as pltpu
from jax.sharding import PartitionSpec as P

BLK = 128


def select_kernel(line, outs, line_ref, table_ref, *refs):
    pieces = refs[: 2 * line - 1]
    out_refs = refs[2 * line - 1 : 2 * line - 1 + outs]
    held, sems = refs[2 * line - 1 + outs :]
    me = line_ref[0]
    per = held.shape[0] // line

    def copy(piece, place):
        return pltpu.make_async_copy(
            pieces[piece], held.at[pl.ds(place * per, per)], sems.at[place]
        )

    def each(action):
        action(copy(0, me))
        for k in range(1, line):

            @pl.when(me >= k)
            def _(k=k):
                action(copy(k, me - k))

            @pl.when(me + k < line)
            def _(k=k):
                action(copy(line - 1 + k, me + k))

    each(lambda c: c.start())
    each(lambda c: c.wait())
    for o, out_ref in enumerate(out_refs):
        count = out_ref.shape[0]

        @pl.loop(0, count, unroll=4)
        def _(i, o=o, out_ref=out_ref, count=count):
            out_ref[i] = held[table_ref[o * count + i]]


def select_tiles(me, table, pieces, outs, line):
    blocks, rows, blk = pieces[0].shape
    count = table.shape[0] // outs
    return pl.pallas_call(
        functools.partial(select_kernel, line, outs),
        out_shape=[jax.ShapeDtypeStruct((count, rows, blk), pieces[0].dtype)] * outs,
        in_specs=[pl.BlockSpec(memory_space=pltpu.SMEM)] * 2
        + [pl.BlockSpec(memory_space=pl.ANY)] * len(pieces),
        out_specs=[pl.BlockSpec(memory_space=pltpu.VMEM)] * outs,
        scratch_shapes=[
            pltpu.VMEM((line * blocks, rows, blk), pieces[0].dtype),
            pltpu.SemaphoreType.DMA((line,)),
        ],
        compiler_params=pltpu.CompilerParams(vmem_limit_bytes=40 << 20),
        name="select_tiles",
    )(me, table, *pieces)


def gram_kernel(parts, inverse, *refs):
    out_ref = refs[-1]
    total = jnp.zeros(out_ref.shape[1:], jnp.float32)
    for ref in refs[:parts]:
        total += lax.dot_general(
            ref[0], ref[1], (((0,), (0,)), ((), ())), preferred_element_type=jnp.float32
        )
    out_ref[0] = total * inverse


def gram_sum(tiles, pairs, inverse):
    _, rows, blk = tiles[0].shape
    return pl.pallas_call(
        functools.partial(gram_kernel, len(tiles), inverse),
        grid=(pairs,),
        out_shape=jax.ShapeDtypeStruct((pairs, blk, blk), jnp.float32),
        in_specs=[pl.BlockSpec((2, rows, blk), lambda p: (p, 0, 0))] * len(tiles),
        out_specs=pl.BlockSpec((1, blk, blk), lambda p: (p, 0, 0)),
        name="gram_sum",
    )(*tiles)


def cross_kernel(parts, inverse, *refs):
    out_ref = refs[-1]
    total = jnp.zeros(out_ref.shape[1:], jnp.float32)
    for left, right in zip(refs[:parts], refs[parts : 2 * parts]):
        total += lax.dot_general(
            left[0], right[0], (((0,), (0,)), ((), ())), preferred_element_type=jnp.float32
        )
    out_ref[0] = total * inverse


def cross_sum(left, right, pairs, inverse):
    _, rows, blk = left[0].shape
    return pl.pallas_call(
        functools.partial(cross_kernel, len(left), inverse),
        grid=(pairs,),
        out_shape=jax.ShapeDtypeStruct((pairs, blk, blk), jnp.float32),
        in_specs=[pl.BlockSpec((1, rows, blk), lambda p: (2 * p, 0, 0))] * len(left)
        + [pl.BlockSpec((1, rows, blk), lambda p: (p, 0, 0))] * len(left),
        out_specs=pl.BlockSpec((1, blk, blk), lambda p: (p, 0, 0)),
        name="cross_sum",
    )(*left, *right)


def body(span_input, span_output, block_pairs):
    tok_count = lax.axis_size("tok")
    feat_count = lax.axis_size("feat")
    tok = lax.axis_index("tok")
    feat = lax.axis_index("feat")
    rows, width = span_input.shape
    inverse = 1.0 / (tok_count * rows)
    pair_dev = block_pairs.shape[0] // (tok_count * feat_count)
    sides = 2 if feat_count % 2 == 0 and rows % 32 == 0 else 1
    line = feat_count // sides
    place, side = feat // sides, feat % sides
    own_blocks = width // BLK
    half = rows // sides

    def blocks_of(array, which):
        part = lax.dynamic_slice_in_dim(array, which * half, half, 0)
        return part.reshape(half, own_blocks, BLK).transpose(1, 0, 2)

    def unit_of(array):
        pieces = [blocks_of(array, side)]
        for d in range(1, sides):
            sent = blocks_of(array, (side + d) % sides)
            perm = [
                (f, f // sides * sides + (f % sides + d) % sides) for f in range(feat_count)
            ]
            pieces.append(lax.ppermute(sent, "feat", perm))
        return jnp.concatenate(pieces, 0) if sides > 1 else pieces[0]

    def gather_line(unit):
        ups, downs = [], []
        up = down = unit
        for k in range(1, line):
            up = lax.ppermute(
                up, "feat",
                [(p * sides + s, (p + 1) * sides + s) for p in range(k - 1, line - 1) for s in range(sides)],
            )
            down = lax.ppermute(
                down, "feat",
                [((p + 1) * sides + s, p * sides + s) for p in range(0, line - k) for s in range(sides)],
            )
            ups.append(up)
            downs.append(down)
        return [unit] + ups + downs

    deltas = [(dt, ds) for dt in range(tok_count) for ds in range(sides)]
    owner = jnp.stack(
        [((tok + dt) % tok_count) * feat_count + place * sides + (side + ds) % sides for dt, ds in deltas]
    )
    listed = jnp.take(
        block_pairs.reshape(tok_count * feat_count, pair_dev, 2), owner, axis=0
    )
    piece = (side - listed // own_blocks % sides) % sides
    slots = listed // (own_blocks * sides) * (own_blocks * sides) + piece * own_blocks + listed % own_blocks
    me = place.reshape(1).astype(jnp.int32)

    def to_owners(tiles):
        got = []
        for (dt, ds), sent in zip(deltas, tiles):
            if dt == 0 and ds == 0:
                got.append(sent)
                continue
            perm = [
                (
                    t * feat_count + f,
                    (t + dt) % tok_count * feat_count + f // sides * sides + (f % sides + ds) % sides,
                )
                for t in range(tok_count)
                for f in range(feat_count)
            ]
            got.append(lax.ppermute(sent, ("tok", "feat"), perm))
        return got

    outs = len(deltas)
    unit_in = unit_of(span_input)
    unit_out = unit_of(span_output)
    line_in = gather_line(unit_in)
    line_out = gather_line(unit_out)
    tiles_in = to_owners(select_tiles(me, slots.reshape(-1), line_in, outs, line))
    tiles_out = to_owners(select_tiles(me, slots[:, :, 1].reshape(-1), line_out, outs, line))
    gram = gram_sum(tiles_in, pair_dev, inverse)
    cross = cross_sum(tiles_in, tiles_out, pair_dev, inverse)
    return gram, cross


def solution(mesh):
    return jax.shard_map(
        body,
        mesh=mesh,
        in_specs=(P("tok", "feat"), P("tok", "feat"), P()),
        out_specs=(P(("tok", "feat"), None, None), P(("tok", "feat"), None, None)),
        check_vma=False,
    )
```

```python
import functools

import jax
import jax.numpy as jnp
from jax import lax
from jax.experimental import pallas as pl
from jax.experimental.pallas import tpu as pltpu
from jax.sharding import PartitionSpec as P

BLK = 128
VMEM_LIMIT = 56 << 20


def select_kernel(offsets, outs, places_ref, table_ref, *refs):
    line = len(offsets)
    pieces, out_refs = refs[:line], refs[line : line + outs]
    held, sems = refs[line + outs :]
    per, rows = held.shape[0] // line, held.shape[1]
    copies = [
        pltpu.make_async_copy(
            piece.at[:, pl.ds(offset, rows), :],
            held.at[pl.ds(places_ref[k] * per, per)],
            sems.at[k],
        )
        for k, (piece, offset) in enumerate(zip(pieces, offsets))
    ]
    for copy in copies:
        copy.start()
    for copy in copies:
        copy.wait()
    for o, out_ref in enumerate(out_refs):
        count = out_ref.shape[0]

        @pl.loop(0, count, unroll=4)
        def _(i, o=o, out_ref=out_ref, count=count):
            out_ref[i] = held[table_ref[o * count + i]]


def select_tiles(places, table, pieces, offsets, rows, outs):
    blocks, _, blk = pieces[0].shape
    dtype = pieces[0].dtype
    return pl.pallas_call(
        functools.partial(select_kernel, offsets, outs),
        out_shape=[jax.ShapeDtypeStruct((table.shape[0] // outs, rows, blk), dtype)] * outs,
        in_specs=[pl.BlockSpec(memory_space=pltpu.SMEM)] * 2
        + [pl.BlockSpec(memory_space=pl.ANY)] * len(pieces),
        out_specs=[pl.BlockSpec(memory_space=pltpu.VMEM)] * outs,
        scratch_shapes=[
            pltpu.VMEM((len(pieces) * blocks, rows, blk), dtype),
            pltpu.SemaphoreType.DMA((len(pieces),)),
        ],
        compiler_params=pltpu.CompilerParams(vmem_limit_bytes=VMEM_LIMIT),
        name="select_tiles",
    )(places, table, *pieces)


def rows_of(refs, parts, group, which, p):
    return jnp.concatenate(
        [ref[k * group + which(p)] for ref, held in zip(refs, parts) for k in held], 0
    )


def gram_kernel(parts, inverse, *refs):
    tiles, out_ref, left_ref = refs[: len(parts)], refs[len(parts)], refs[len(parts) + 1]
    pairs = out_ref.shape[0]

    @pl.loop(0, pairs)
    def _(p):
        left = rows_of(tiles, parts, 2 * pairs, lambda p: 2 * p, p).T
        right = rows_of(tiles, parts, 2 * pairs, lambda p: 2 * p + 1, p)
        left_ref[p] = left
        out_ref[p] = jnp.dot(left, right, preferred_element_type=jnp.float32) * inverse


def cross_kernel(parts, inverse, left_ref, *refs):
    tiles, out_ref = refs[: len(parts)], refs[len(parts)]
    pairs = out_ref.shape[0]

    @pl.loop(0, pairs)
    def _(p):
        right = rows_of(tiles, parts, pairs, lambda p: p, p)
        out_ref[p] = jnp.dot(left_ref[p], right, preferred_element_type=jnp.float32) * inverse


def sum_call(kernel, operands, outs, name):
    return pl.pallas_call(
        kernel,
        out_shape=outs,
        in_specs=[pl.BlockSpec(memory_space=pltpu.VMEM)] * len(operands),
        out_specs=[pl.BlockSpec(memory_space=pltpu.VMEM)] * len(outs),
        compiler_params=pltpu.CompilerParams(vmem_limit_bytes=VMEM_LIMIT),
        name=name,
    )(*operands)


def after(values, done):
    return lax.optimization_barrier((values, done))


def body(span_input, span_output, block_pairs):
    tok_count = lax.axis_size("tok")
    feat_count = lax.axis_size("feat")
    tok = lax.axis_index("tok")
    feat = lax.axis_index("feat")
    rows, width = span_input.shape
    inverse = 1.0 / (tok_count * rows)
    pairs = block_pairs.shape[0] // (tok_count * feat_count)
    own_blocks = width // BLK
    sides = 2 if feat_count % 2 == 0 and rows % 64 == 0 else 1
    line = feat_count // sides
    place, side = feat // sides, feat % sides
    chunks = 2 if rows % (32 * sides) == 0 else 1
    half = rows // sides
    chunk = half // chunks
    paired = line & (line - 1) == 0

    def blocks_of(array, which, start, count):
        part = lax.dynamic_slice_in_dim(array, which * half + start, count, 0)
        return part.reshape(count, own_blocks, BLK).transpose(1, 0, 2)

    def from_sides(array, start, count):
        return [
            lax.ppermute(
                blocks_of(array, (side + d) % sides, start, count), "feat",
                [(f, f // sides * sides + (f % sides + d) % sides) for f in range(feat_count)],
            )
            for d in range(1, sides)
        ]

    def at_place(p, k):
        return p ^ k if paired else (p + k) % line

    def hop(piece, k):
        return lax.ppermute(piece, "feat", [
            (f, at_place(f // sides, k) * sides + f % sides) for f in range(feat_count)
        ])

    def far_hops(unit):
        held = {0: unit}
        if not paired:
            held.update({k: hop(unit, k) for k in range(1, line)})
            return held
        k = line // 2
        while k > 1:
            held.update({m ^ k: hop(piece, k) for m, piece in list(held.items())})
            k //= 2
        if line > 1:
            held[1] = hop(unit, 1)
        return held

    def last_hops(held):
        return {m ^ 1: hop(held[m], 1) for m in held if m > 1 and m ^ 1 not in held}

    places = jnp.stack([at_place(place, k) if paired else (place - k) % line for k in range(line)])
    places = places.astype(jnp.int32)

    cores = 2 if tok_count % 2 == 0 else 1
    chips = [(dt, ds) for dt in range(0, tok_count, cores) for ds in range(sides)]

    def other(t, c):
        return t + c * (1 - 2 * (t % 2))

    owner = jnp.stack([
        other((tok + dt) % tok_count, c) * feat_count + place * sides + (side + ds) % sides
        for dt, ds in chips
        for c in range(cores)
    ])
    listed = jnp.take(block_pairs.reshape(tok_count * feat_count, pairs, 2), owner, axis=0)
    stream = (side - listed // own_blocks % sides) % sides
    slots = listed // (own_blocks * sides) * (own_blocks * sides) + stream * own_blocks + listed % own_blocks

    def send(tiles, chip, c):
        dt, ds = chip
        return lax.ppermute(tiles, ("tok", "feat"), [
            (
                t * feat_count + f,
                other((t + dt) % tok_count, c) * feat_count + f // sides * sides + (f % sides + ds) % sides,
            )
            for t in range(tok_count)
            for f in range(feat_count)
        ])

    def to_owners(tiles):
        got = [tiles[0]] + [send(sent, chip, 0) for sent, chip in zip(tiles[1:], chips[1:])]
        if cores > 1:
            own = tiles[0].shape[0] // cores
            got.append(send(jnp.concatenate([g[own:] for g in got], 0), (0, 0), 1))
        return got

    parts = [(0,)] * len(chips) + [tuple(range(len(chips)))] * (cores > 1)

    brought = [from_sides(span_input, i * chunk, chunk) for i in range(chunks)]
    others_out = from_sides(span_output, 0, half)
    own_out = blocks_of(span_output, side, 0, half)
    tiles_in = []
    held = None
    for i in range(chunks):
        unit = jnp.concatenate([blocks_of(span_input, side, i * chunk, chunk)] + brought[i], 0)
        if held:
            unit, held = after(unit, held)
        ahead = held
        held = far_hops(unit)
        if ahead:
            whole = {**ahead, **last_hops(ahead)}
            picked = select_tiles(
                places, slots.reshape(-1), [whole[k] for k in range(line)], (0,) * line, chunk, len(chips)
            )
            tiles_in += to_owners(picked)
    own_out, held = after(own_out, held)
    whole = {**held, **last_hops(held)}
    picked = select_tiles(
        places, slots.reshape(-1), [whole[k] for k in range(line)], (0,) * line, chunk, len(chips)
    )
    tiles_in += to_owners(picked)

    held = far_hops(jnp.concatenate([own_out] + others_out, 0))
    tiles_out = []
    for i in range(chunks):
        last = last_hops({k: h[:, i * chunk : (i + 1) * chunk] for k, h in held.items()})
        pieces = [last[k] if k in last else held[k] for k in range(line)]
        offsets = tuple(0 if k in last else i * chunk for k in range(line))
        picked = select_tiles(places, slots[:, :, 1].reshape(-1), pieces, offsets, chunk, len(chips))
        tiles_out += to_owners(picked)

    gram_shape = jax.ShapeDtypeStruct((pairs, BLK, BLK), jnp.float32)
    gram, left = sum_call(
        functools.partial(gram_kernel, parts * chunks, inverse), tiles_in,
        [gram_shape, jax.ShapeDtypeStruct((pairs, BLK, tok_count * rows), span_input.dtype)],
        "gram_sum",
    )
    (cross,) = sum_call(
        functools.partial(cross_kernel, parts * chunks, inverse), [left] + tiles_out,
        [gram_shape], "cross_sum",
    )
    return gram, cross


def solution(mesh):
    return jax.shard_map(
        body,
        mesh=mesh,
        in_specs=(P("tok", "feat"), P("tok", "feat"), P()),
        out_specs=(P(("tok", "feat"), None, None), P(("tok", "feat"), None, None)),
        check_vma=False,
    )
```

```python
import functools

import jax
import jax.numpy as jnp
from jax import lax
from jax.experimental import pallas as pl
from jax.experimental.pallas import tpu as pltpu
from jax.sharding import PartitionSpec as P

BLK = 128
VMEM_LIMIT = 56 << 20
CROSS_LIMIT = 24 << 20


def select_kernel(line, groups, places_ref, table_ref, *refs):
    pieces, (out_ref, held, stage, sems, out_sems) = refs[:-5], refs[-5:]
    streams = len(pieces) // line
    per = held.shape[0] // len(pieces)
    copies = [
        pltpu.make_async_copy(
            piece, held.at[pl.ds((places_ref[n % line] * streams + n // line) * per, per)], sems.at[n]
        )
        for n, piece in enumerate(pieces)
    ]
    for copy in copies:
        copy.start()
    for copy in copies:
        copy.wait()
    count = stage.shape[0] // groups
    copies = []
    for g in range(groups):

        @pl.loop(0, count, unroll=4)
        def _(i, g=g):
            stage[g * count + i] = held[table_ref[g * count + i]]

        part = pl.ds(g * count, count)
        copies.append(pltpu.make_async_copy(stage.at[part], out_ref.at[part], out_sems.at[g]))
        copies[-1].start()
    for copy in copies:
        copy.wait()


def select_tiles(places, table, streams, groups):
    pieces = [piece for stream in streams for piece in stream]
    blocks, rows, blk = pieces[0].shape
    dtype = pieces[0].dtype
    out_shape = (table.shape[0], rows, blk)
    return pl.pallas_call(
        functools.partial(select_kernel, len(streams[0]), groups),
        out_shape=jax.ShapeDtypeStruct(out_shape, dtype),
        in_specs=[pl.BlockSpec(memory_space=pltpu.SMEM)] * 2
        + [pl.BlockSpec(memory_space=pl.ANY)] * len(pieces),
        out_specs=pl.BlockSpec(memory_space=pl.ANY),
        scratch_shapes=[
            pltpu.VMEM((len(pieces) * blocks, rows, blk), dtype),
            pltpu.VMEM(out_shape, dtype),
            pltpu.SemaphoreType.DMA((len(pieces),)),
            pltpu.SemaphoreType.DMA((groups,)),
        ],
        compiler_params=pltpu.CompilerParams(vmem_limit_bytes=VMEM_LIMIT),
        name="select_tiles",
    )(places, table, *pieces)


def rows_of(ref, group, which):
    return jnp.concatenate([ref[k + which] for k in range(0, ref.shape[0], group)], 0)


def gram_kernel(inverse, tiles, out_ref, left_ref):
    pairs = out_ref.shape[0]

    @pl.loop(0, pairs, unroll=2)
    def _(p):
        left = rows_of(tiles, 2 * pairs, 2 * p).T
        right = rows_of(tiles, 2 * pairs, 2 * p + 1)
        left_ref[p] = left
        out_ref[p] = jnp.dot(left, right, preferred_element_type=jnp.float32) * inverse


def cross_kernel(inverse, left_ref, tiles, out_ref):
    pairs = out_ref.shape[0]

    @pl.loop(0, pairs, unroll=4)
    def _(p):
        right = rows_of(tiles, pairs, p)
        out_ref[p] = jnp.dot(left_ref[p], right, preferred_element_type=jnp.float32) * inverse


def sum_call(kernel, operands, outs, name, vmem):
    return pl.pallas_call(
        kernel,
        out_shape=outs,
        in_specs=[pl.BlockSpec(memory_space=pltpu.VMEM)] * len(operands),
        out_specs=[pl.BlockSpec(memory_space=pltpu.VMEM)] * len(outs),
        compiler_params=pltpu.CompilerParams(vmem_limit_bytes=vmem),
        name=name,
    )(*operands)


def after(values, done):
    return lax.optimization_barrier((values, done))


def body(span_input, span_output, block_pairs):
    tok_count = lax.axis_size("tok")
    feat_count = lax.axis_size("feat")
    feat = lax.axis_index("feat")
    rows, width = span_input.shape
    inverse = 1.0 / (tok_count * rows)
    pairs = block_pairs.shape[0] // (tok_count * feat_count)
    own_blocks = width // BLK
    sides = 2 if feat_count % 2 == 0 and rows % 32 == 0 else 1
    line = feat_count // sides
    place, side = feat // sides, feat % sides
    part = rows // sides
    paired = line & (line - 1) == 0

    def blocks_of(array, which):
        taken = lax.dynamic_slice_in_dim(array, which * part, part, 0)
        return taken.reshape(part, own_blocks, BLK).transpose(1, 0, 2)

    def from_sides(array):
        return [
            lax.ppermute(
                blocks_of(array, (side + d) % sides), "feat",
                [(f, f // sides * sides + (f % sides + d) % sides) for f in range(feat_count)],
            )
            for d in range(1, sides)
        ]

    def at_place(p, k):
        return p ^ k if paired else (p + k) % line

    def hop(piece, k):
        return lax.ppermute(piece, "feat", [
            (f, at_place(f // sides, k) * sides + f % sides) for f in range(feat_count)
        ])

    def far_hops(unit):
        held = {0: unit}
        if not paired:
            held.update({k: hop(unit, k) for k in range(1, line)})
            return held
        k = line // 2
        while k > 1:
            held.update({m ^ k: hop(piece, k) for m, piece in list(held.items())})
            k //= 2
        if line > 1:
            held[1] = hop(unit, 1)
        return held

    def last_hops(held):
        return {m ^ 1: hop(held[m], 1) for m in held if m > 1 and m ^ 1 not in held}

    def in_order(held):
        return [held[k] for k in range(line)]

    places = jnp.stack([at_place(place, k) if paired else (place - k) % line for k in range(line)])
    places = places.astype(jnp.int32)

    owners = [(t, s) for t in range(tok_count) for s in range(sides)]
    groups = [[t * feat_count + p * sides + s for t, s in owners] for p in range(line)]
    listed = block_pairs.reshape(tok_count, line, sides * pairs, 2)
    listed = lax.dynamic_index_in_dim(listed, place, 1, keepdims=False).reshape(-1, 2)
    stream = (side - listed // own_blocks % sides) % sides
    slots = listed // (own_blocks * sides) * (own_blocks * sides) + stream * own_blocks + listed % own_blocks

    def to_owners(tiles):
        return lax.all_to_all(
            tiles, ("tok", "feat"), split_axis=0, concat_axis=0, axis_index_groups=groups, tiled=True
        )

    own_out = blocks_of(span_output, side)
    others_in, others_out = from_sides(span_input), from_sides(span_output)
    streams_in = [far_hops(blocks_of(span_input, side))]
    if sides > 1:
        others_in, streams_in[0][1] = after(others_in, streams_in[0][1])
        streams_in += [far_hops(other) for other in others_in]
    streams_in[0].update(last_hops(streams_in[0]))
    (own_out, others_out), streams_in[-1] = after((own_out, others_out), streams_in[-1])
    for held in streams_in[1:]:
        held.update(last_hops(held))
    streams_out = [far_hops(unit) for unit in [own_out] + others_out]
    picked = select_tiles(places, slots.reshape(-1), [in_order(h) for h in streams_in], len(owners))
    tiles_in = to_owners(picked)
    for held in streams_out:
        held.update(last_hops(held))
    picked = select_tiles(places, slots[:, 1], [in_order(h) for h in streams_out], len(owners))
    tiles_out = to_owners(picked)

    gram_shape = jax.ShapeDtypeStruct((pairs, BLK, BLK), jnp.float32)
    left_shape = jax.ShapeDtypeStruct((pairs, BLK, tok_count * rows), span_input.dtype)
    gram, left = sum_call(
        functools.partial(gram_kernel, inverse), [tiles_in], [gram_shape, left_shape], "gram_sum", VMEM_LIMIT
    )
    (cross,) = sum_call(
        functools.partial(cross_kernel, inverse), [left, tiles_out], [gram_shape], "cross_sum", CROSS_LIMIT
    )
    return gram, cross


def solution(mesh):
    return jax.shard_map(
        body,
        mesh=mesh,
        in_specs=(P("tok", "feat"), P("tok", "feat"), P()),
        out_specs=(P(("tok", "feat"), None, None), P(("tok", "feat"), None, None)),
        check_vma=False,
    )
```

```python
import functools

import jax
import jax.numpy as jnp
from jax import lax
from jax.experimental import pallas as pl
from jax.experimental.pallas import tpu as pltpu
from jax.sharding import PartitionSpec as P

BLK = 128
SELECT_LIMIT = 56 << 20
SUM_LIMIT = 20 << 20


def select_kernel(where, groups, outs, places_ref, table_ref, *refs):
    pieces, out_refs, (held, stage, sems, out_sems) = refs[: -4 - outs], refs[-4 - outs : -4], refs[-4:]
    per = held.shape[0] // places_ref.shape[0]
    copies = [
        pltpu.make_async_copy(
            piece, held.at[pl.ds(places_ref[k] * per + first, piece.shape[0])], sems.at[n]
        )
        for n, (piece, (k, first)) in enumerate(zip(pieces, where))
    ]
    for copy in copies:
        copy.start()
    for copy in copies:
        copy.wait()
    count = stage.shape[0] // groups
    copies = []
    for g in range(groups):

        @pl.loop(0, count, unroll=4)
        def _(i, g=g):
            stage[g * count + i] = held[table_ref[g * count + i]]

        part = pl.ds(g * count, count)
        out = out_refs[g] if outs > 1 else out_refs[0].at[part]
        copies.append(pltpu.make_async_copy(stage.at[part], out, out_sems.at[g]))
        copies[-1].start()
    for copy in copies:
        copy.wait()


def late_kernel(k, first, per, outs, places_ref, table_ref, piece, *refs):
    out_refs, (held, sem, out_sem) = refs[outs:-3], refs[-3:]
    load = pltpu.make_async_copy(piece, held, sem)
    load.start()
    blocks = held.shape[0]
    begin = places_ref[k] * per + first
    load.wait()
    sent = 0
    for g, out_ref in enumerate(out_refs):
        count = out_ref.shape[0]

        def put(i, sent, g=g, out_ref=out_ref, count=count):
            slot = table_ref[g * count + i] - begin
            mine = jnp.logical_and(slot >= 0, slot < blocks)

            @pl.when(mine)
            def _():
                pltpu.make_async_copy(held.at[slot], out_ref.at[i], out_sem).start()

            return sent + mine.astype(jnp.int32)

        sent = lax.fori_loop(0, count, put, sent)

    @pl.loop(0, sent)
    def _(i):
        pltpu.make_async_copy(held.at[0], out_refs[0].at[0], out_sem).wait()


def select_tiles(places, table, pieces, groups, apart, late=None):
    early = pieces[:-1] if late else pieces
    where, arrays = [w for w, _ in early], [array for _, array in early]
    _, rows, blk = arrays[0].shape
    dtype = arrays[0].dtype
    count = table.shape[0]
    outs = groups if apart else 1
    shapes = [jax.ShapeDtypeStruct((count // outs, rows, blk), dtype)] * outs
    total = sum(array.shape[0] for _, array in pieces)
    picked = pl.pallas_call(
        functools.partial(select_kernel, where, groups, outs),
        out_shape=shapes,
        in_specs=[pl.BlockSpec(memory_space=pltpu.SMEM)] * 2
        + [pl.BlockSpec(memory_space=pl.ANY)] * len(arrays),
        out_specs=[pl.BlockSpec(memory_space=pl.ANY)] * outs,
        scratch_shapes=[
            pltpu.VMEM((total, rows, blk), dtype),
            pltpu.VMEM((count, rows, blk), dtype),
            pltpu.SemaphoreType.DMA((len(arrays),)),
            pltpu.SemaphoreType.DMA((groups,)),
        ],
        compiler_params=pltpu.CompilerParams(vmem_limit_bytes=SELECT_LIMIT),
        name="select_tiles",
    )(places, table, *arrays)
    if not late:
        return picked
    (k, first), piece = pieces[-1]
    return pl.pallas_call(
        functools.partial(late_kernel, k, first, total // places.shape[0], outs),
        out_shape=shapes,
        in_specs=[pl.BlockSpec(memory_space=pltpu.SMEM)] * 2
        + [pl.BlockSpec(memory_space=pl.ANY)] * (1 + outs),
        out_specs=[pl.BlockSpec(memory_space=pl.ANY)] * outs,
        scratch_shapes=[
            pltpu.VMEM(piece.shape, dtype),
            pltpu.SemaphoreType.DMA,
            pltpu.SemaphoreType.DMA,
        ],
        input_output_aliases={3 + i: i for i in range(outs)},
        compiler_params=pltpu.CompilerParams(vmem_limit_bytes=SELECT_LIMIT),
        name="late_tiles",
    )(places, table, piece, *picked)


def rows_in_order(order_ref, tiles, group, which, rows):
    return jnp.concatenate(
        [tiles[order_ref[d] * group + which, rows] for d in range(order_ref.shape[0])], 0
    )


def left_kernel(chunks, order_ref, tiles, *left_refs):
    pairs = left_refs[0].shape[0]
    chunk = tiles.shape[1] // chunks

    @pl.loop(0, pairs, unroll=2)
    def _(p):
        for c, left_ref in enumerate(left_refs):
            rows = slice(c * chunk, (c + 1) * chunk)
            left_ref[p] = rows_in_order(order_ref, tiles, 2 * pairs, 2 * p, rows).T


def gram_kernel(inverse, chunks, order_ref, *refs):
    lefts, (tiles, out_ref) = refs[:chunks], refs[chunks:]
    pairs = out_ref.shape[0]
    chunk = tiles.shape[1] // chunks

    @pl.loop(0, pairs, unroll=2)
    def _(p):
        total = jnp.zeros(out_ref.shape[1:], jnp.float32)
        for c, left_ref in enumerate(lefts):
            rows = slice(c * chunk, (c + 1) * chunk)
            right = rows_in_order(order_ref, tiles, 2 * pairs, 2 * p + 1, rows)
            total += jnp.dot(left_ref[p], right, preferred_element_type=jnp.float32)
        out_ref[p] = total * inverse


def cross_kernel(inverse, parts, left_ref, *refs):
    tiles, before, out_ref = refs[:parts], refs[parts:-1], refs[-1]
    pairs = out_ref.shape[0]

    @pl.loop(0, pairs, unroll=4)
    def _(p):
        right = jnp.concatenate([ref[p] for ref in tiles], 0)
        total = jnp.dot(left_ref[p], right, preferred_element_type=jnp.float32) * inverse
        out_ref[p] = total + before[0][p] if before else total


def sum_call(kernel, operands, outs, name):
    return pl.pallas_call(
        kernel,
        out_shape=outs,
        in_specs=[
            pl.BlockSpec(memory_space=pltpu.SMEM if operand.ndim == 1 else pltpu.VMEM)
            for operand in operands
        ],
        out_specs=[pl.BlockSpec(memory_space=pltpu.VMEM)] * len(outs),
        compiler_params=pltpu.CompilerParams(vmem_limit_bytes=SUM_LIMIT),
        name=name,
    )(*operands)


def after(values, done):
    return lax.optimization_barrier((values, done))


def body(span_input, span_output, block_pairs):
    tok_count = lax.axis_size("tok")
    feat_count = lax.axis_size("feat")
    tok = lax.axis_index("tok")
    feat = lax.axis_index("feat")
    rows, width = span_input.shape
    inverse = 1.0 / (tok_count * rows)
    pairs = block_pairs.shape[0] // (tok_count * feat_count)
    own_blocks = width // BLK
    sides = 2 if feat_count % 2 == 0 and rows % 32 == 0 else 1
    line = feat_count // sides
    place, side = feat // sides, feat % sides
    part = rows // sides
    chunks = 2 if part % 32 == 0 else 1
    chunk = part // chunks
    paired = line & (line - 1) == 0

    def blocks_of(array, which):
        taken = lax.dynamic_slice_in_dim(array, which * part, part, 0)
        return taken.reshape(part, own_blocks, BLK).transpose(1, 0, 2)

    def from_sides(array):
        return [
            lax.ppermute(
                blocks_of(array, (side + d) % sides), "feat",
                [(f, f // sides * sides + (f % sides + d) % sides) for f in range(feat_count)],
            )
            for d in range(1, sides)
        ]

    def at_place(p, k):
        return p ^ k if paired else (p + k) % line

    def hop(piece, k):
        return lax.ppermute(piece, "feat", [
            (f, at_place(f // sides, k) * sides + f % sides) for f in range(feat_count)
        ])

    def far_hops(unit):
        held = {0: unit}
        if not paired:
            held.update({k: hop(unit, k) for k in range(1, line)})
            return held
        k = line // 2
        while k > 1:
            held.update({m ^ k: hop(piece, k) for m, piece in list(held.items())})
            k //= 2
        if line > 1:
            held[1] = hop(unit, 1)
        return held

    def last_hops(held):
        return {m ^ 1: hop(held[m], 1) for m in held if m > 1 and m ^ 1 not in held}

    def pieces_of(streams):
        pieces, first = [], 0
        for held in streams:
            pieces += [((k, first), held[k]) for k in range(line)]
            first += held[0].shape[0]
        return pieces

    places = jnp.stack([at_place(place, k) if paired else (place - k) % line for k in range(line)])
    places = places.astype(jnp.int32)

    owners = [(t, s) for t in range(tok_count) for s in range(sides)]
    groups = [[t * feat_count + p * sides + s for t, s in owners] for p in range(line)]
    listed = block_pairs.reshape(tok_count, line, sides * pairs, 2)
    listed = lax.dynamic_index_in_dim(listed, place, 1, keepdims=False).reshape(len(owners), pairs, 2)
    stream = (side - listed // own_blocks % sides) % sides
    slots = listed // (own_blocks * sides) * (own_blocks * sides) + stream * own_blocks + listed % own_blocks
    away = jnp.stack([
        (tok + d // sides) % tok_count * sides + (side + d) % sides for d in range(len(owners))
    ])
    right_slots = jnp.take(slots[:, :, 1], away, axis=0).reshape(-1)
    sources = jnp.stack([
        (tok - d // sides) % tok_count * sides + (side - d) % sides for d in range(len(owners))
    ]).astype(jnp.int32)

    def to_owners(tiles):
        return lax.all_to_all(
            tiles, ("tok", "feat"), split_axis=0, concat_axis=0, axis_index_groups=groups, tiled=True
        )

    def to_owner(tiles, d):
        if d == 0:
            return tiles
        perm = []
        for t, s in owners:
            to_t, to_s = (t + d // sides) % tok_count, (s + d) % sides
            perm += [
                (t * feat_count + p * sides + s, to_t * feat_count + p * sides + to_s) for p in range(line)
            ]
        return lax.ppermute(tiles, ("tok", "feat"), perm)

    own_out = blocks_of(span_output, side)
    others_in, others_out = from_sides(span_input), from_sides(span_output)
    streams_in = [far_hops(blocks_of(span_input, side))]
    if sides > 1:
        others_in, streams_in[0][1] = after(others_in, streams_in[0][1])
        streams_in += [far_hops(other) for other in others_in]
    streams_in[0].update(last_hops(streams_in[0]))
    unit = jnp.concatenate([own_out] + others_out, 0)
    units = [unit[:, c * chunk : (c + 1) * chunk] for c in range(chunks)]
    units, streams_in[-1] = after(units, streams_in[-1])
    for held in streams_in[1:]:
        held.update(last_hops(held))
    chunks_out = [far_hops(unit) for unit in units]
    (picked,) = select_tiles(places, slots.reshape(-1), pieces_of(streams_in), len(owners), False, True)
    tiles_in = to_owners(picked)
    for held in chunks_out:
        held.update(last_hops(held))

    gram_shape = jax.ShapeDtypeStruct((pairs, BLK, BLK), jnp.float32)
    left_shape = jax.ShapeDtypeStruct((pairs, BLK, len(owners) * chunk), span_input.dtype)
    lefts = sum_call(
        functools.partial(left_kernel, chunks), [sources, tiles_in], [left_shape] * chunks, "left_tiles"
    )
    cross = []
    for c, held in enumerate(chunks_out):
        final = c + 1 == chunks
        picked = select_tiles(places, right_slots, pieces_of([held]), len(owners), True, not final)
        if final:
            picked, lefts = after(picked, lefts)
        got = [to_owner(tiles, d) for d, tiles in enumerate(picked)]
        if final:
            (gram,) = sum_call(
                functools.partial(gram_kernel, inverse, chunks), [sources] + list(lefts) + [tiles_in],
                [gram_shape], "gram_sum",
            )
            cross, gram = after(list(cross), gram)
        cross = sum_call(
            functools.partial(cross_kernel, inverse, len(got)), [lefts[c]] + got + list(cross),
            [gram_shape], "cross_sum",
        )
    (cross,) = cross
    return gram, cross


def solution(mesh):
    return jax.shard_map(
        body,
        mesh=mesh,
        in_specs=(P("tok", "feat"), P("tok", "feat"), P()),
        out_specs=(P(("tok", "feat"), None, None), P(("tok", "feat"), None, None)),
        check_vma=False,
    )
```

```python
import functools

import jax
import jax.numpy as jnp
from jax import lax
from jax.experimental import pallas as pl
from jax.experimental.pallas import tpu as pltpu
from jax.sharding import PartitionSpec as P

BLK = 128
SELECT_LIMIT = 56 << 20
SUM_LIMIT = 20 << 20


def select_kernel(where, groups, outs, late, places_ref, table_ref, *refs):
    arrays = len(where)
    pieces, out_refs, rest = refs[:arrays], refs[arrays : arrays + outs], refs[arrays + outs :]
    list_ref, held, stage, sems, out_sems = rest
    per = held.shape[0] // places_ref.shape[0]
    copies = [
        pltpu.make_async_copy(
            piece, held.at[pl.ds(places_ref[k] * per + first, piece.shape[0])], sems.at[n]
        )
        for n, (piece, (k, first)) in enumerate(zip(pieces, where))
    ]
    for copy in copies:
        copy.start()
    k, first, blocks = late
    begin = places_ref[k] * per + first

    def note(i, found):
        slot = table_ref[i] - begin
        list_ref[found + 1] = i
        return found + jnp.logical_and(slot >= 0, slot < blocks).astype(jnp.int32)

    list_ref[0] = lax.fori_loop(0, table_ref.shape[0], note, 0, unroll=4)
    for copy in copies:
        copy.wait()
    count = stage.shape[0] // groups
    copies = []
    for g in range(groups):

        @pl.loop(0, count, unroll=4)
        def _(i, g=g):
            stage[g * count + i] = held[table_ref[g * count + i]]

        part = pl.ds(g * count, count)
        out = out_refs[g] if outs > 1 else out_refs[0].at[part]
        copies.append(pltpu.make_async_copy(stage.at[part], out, out_sems.at[g]))
        copies[-1].start()
    for copy in copies:
        copy.wait()


def late_kernel(k, first, per, outs, places_ref, table_ref, list_ref, piece, *refs):
    out_refs, (held, sem, out_sem) = refs[outs:-3], refs[-3:]
    load = pltpu.make_async_copy(piece, held, sem)
    load.start()
    load.wait()
    begin = places_ref[k] * per + first
    count = out_refs[0].shape[0]
    found = list_ref[0]

    @pl.loop(0, found)
    def _(n):
        i = list_ref[n + 1]
        source = held.at[table_ref[i] - begin]
        if outs == 1:
            pltpu.make_async_copy(source, out_refs[0].at[i], out_sem).start()
        for g in range(outs if outs > 1 else 0):

            @pl.when(i // count == g)
            def _(g=g):
                pltpu.make_async_copy(source, out_refs[g].at[i % count], out_sem).start()

    @pl.loop(0, found)
    def _(n):
        pltpu.make_async_copy(held.at[0], out_refs[0].at[0], out_sem).wait()


def select_early(places, table, pieces, groups, apart):
    total = sum(array.shape[0] for _, array in pieces)
    (k, first), last = pieces[-1]
    where, arrays = [w for w, _ in pieces[:-1]], [array for _, array in pieces[:-1]]
    blocks, rows, blk = last.shape
    count = table.shape[0]
    outs = groups if apart else 1
    picked = pl.pallas_call(
        functools.partial(select_kernel, where, groups, outs, (k, first, blocks)),
        out_shape=[jax.ShapeDtypeStruct((count // outs, rows, blk), last.dtype)] * outs
        + [jax.ShapeDtypeStruct((count + 2,), jnp.int32)],
        in_specs=[pl.BlockSpec(memory_space=pltpu.SMEM)] * 2
        + [pl.BlockSpec(memory_space=pl.ANY)] * len(arrays),
        out_specs=[pl.BlockSpec(memory_space=pl.ANY)] * outs + [pl.BlockSpec(memory_space=pltpu.SMEM)],
        scratch_shapes=[
            pltpu.VMEM((total, rows, blk), last.dtype),
            pltpu.VMEM((count, rows, blk), last.dtype),
            pltpu.SemaphoreType.DMA((len(arrays),)),
            pltpu.SemaphoreType.DMA((groups,)),
        ],
        compiler_params=pltpu.CompilerParams(vmem_limit_bytes=SELECT_LIMIT),
        name="select_tiles",
    )(places, table, *arrays)
    return list(picked)


def select_late(places, table, pieces, picked):
    *picked, listed = picked
    (k, first), piece = pieces[-1]
    outs = len(picked)
    per = sum(array.shape[0] for _, array in pieces) // places.shape[0]
    return pl.pallas_call(
        functools.partial(late_kernel, k, first, per, outs),
        out_shape=[jax.ShapeDtypeStruct(p.shape, p.dtype) for p in picked],
        in_specs=[pl.BlockSpec(memory_space=pltpu.SMEM)] * 3
        + [pl.BlockSpec(memory_space=pl.ANY)] * (1 + outs),
        out_specs=[pl.BlockSpec(memory_space=pl.ANY)] * outs,
        scratch_shapes=[
            pltpu.VMEM(piece.shape, piece.dtype),
            pltpu.SemaphoreType.DMA,
            pltpu.SemaphoreType.DMA,
        ],
        input_output_aliases={4 + i: i for i in range(outs)},
        compiler_params=pltpu.CompilerParams(vmem_limit_bytes=SELECT_LIMIT),
        name="late_tiles",
    )(places, table, listed, piece, *picked)


def rows_in_order(order_ref, tiles, p, rows):
    return jnp.concatenate(
        [tiles[order_ref[d], p, 0, rows] for d in range(order_ref.shape[0])], 0
    )


def left_kernel(chunks, order_ref, tiles, *left_refs):
    chunk = tiles.shape[3] // chunks
    for p in range(tiles.shape[1]):
        for c, left_ref in enumerate(left_refs):
            left_ref[p] = rows_in_order(order_ref, tiles, p, slice(c * chunk, (c + 1) * chunk)).T


def gram_kernel(inverse, chunks, order_ref, *refs):
    lefts, (tiles, out_ref) = refs[:chunks], refs[chunks:]
    chunk = tiles.shape[3] // chunks
    for p in range(tiles.shape[1]):
        total = jnp.zeros(out_ref.shape[1:], jnp.float32)
        for c, left_ref in enumerate(lefts):
            right = rows_in_order(order_ref, tiles, p, slice(c * chunk, (c + 1) * chunk))
            total += jnp.dot(left_ref[p], right, preferred_element_type=jnp.float32)
        out_ref[p] = total * inverse


def pairs_call(kernel, order, lefts, tiles, which, outs, name):
    groups, pairs, _, rows, blk = tiles.shape
    step = pairs // 2 if pairs % 2 == 0 else pairs

    def some(array):
        return pl.BlockSpec((step,) + array.shape[1:], lambda p: (p, 0, 0))

    return pl.pallas_call(
        kernel,
        grid=(pairs // step,),
        out_shape=outs,
        in_specs=[pl.BlockSpec(memory_space=pltpu.SMEM)]
        + [some(left) for left in lefts]
        + [pl.BlockSpec((groups, step, 1, rows, blk), lambda p: (0, p, which, 0, 0))],
        out_specs=[some(out) for out in outs],
        compiler_params=pltpu.CompilerParams(vmem_limit_bytes=SUM_LIMIT),
        name=name,
    )(order, *lefts, tiles)


def cross_kernel(inverse, parts, left_ref, *refs):
    tiles, before, out_ref = refs[:parts], refs[parts:-1], refs[-1]
    pairs = out_ref.shape[0]

    @pl.loop(0, pairs, unroll=4)
    def _(p):
        right = jnp.concatenate([ref[p] for ref in tiles], 0)
        total = jnp.dot(left_ref[p], right, preferred_element_type=jnp.float32) * inverse
        out_ref[p] = total + before[0][p] if before else total


def sum_call(kernel, operands, outs, name):
    return pl.pallas_call(
        kernel,
        out_shape=outs,
        in_specs=[
            pl.BlockSpec(memory_space=pltpu.SMEM if operand.ndim == 1 else pltpu.VMEM)
            for operand in operands
        ],
        out_specs=[pl.BlockSpec(memory_space=pltpu.VMEM)] * len(outs),
        compiler_params=pltpu.CompilerParams(vmem_limit_bytes=SUM_LIMIT),
        name=name,
    )(*operands)


def after(values, done):
    return lax.optimization_barrier((values, done))


def body(span_input, span_output, block_pairs):
    tok_count = lax.axis_size("tok")
    feat_count = lax.axis_size("feat")
    tok = lax.axis_index("tok")
    feat = lax.axis_index("feat")
    rows, width = span_input.shape
    inverse = 1.0 / (tok_count * rows)
    pairs = block_pairs.shape[0] // (tok_count * feat_count)
    own_blocks = width // BLK
    sides = 2 if feat_count % 2 == 0 and rows % 32 == 0 else 1
    line = feat_count // sides
    place, side = feat // sides, feat % sides
    part = rows // sides
    chunks = 2 if part % 32 == 0 else 1
    chunk = part // chunks
    paired = line & (line - 1) == 0

    def blocks_of(array, which):
        taken = lax.dynamic_slice_in_dim(array, which * part, part, 0)
        return taken.reshape(part, own_blocks, BLK).transpose(1, 0, 2)

    def from_sides(array):
        return [
            lax.ppermute(
                blocks_of(array, (side + d) % sides), "feat",
                [(f, f // sides * sides + (f % sides + d) % sides) for f in range(feat_count)],
            )
            for d in range(1, sides)
        ]

    def at_place(p, k):
        return p ^ k if paired else (p + k) % line

    def hop(piece, k):
        return lax.ppermute(piece, "feat", [
            (f, at_place(f // sides, k) * sides + f % sides) for f in range(feat_count)
        ])

    def far_hops(unit):
        held = {0: unit}
        if not paired:
            held.update({k: hop(unit, k) for k in range(1, line)})
            return held
        k = line // 2
        while k > 1:
            held.update({m ^ k: hop(piece, k) for m, piece in list(held.items())})
            k //= 2
        if line > 1:
            held[1] = hop(unit, 1)
        return held

    def last_hops(held):
        return {m ^ 1: hop(held[m], 1) for m in held if m > 1 and m ^ 1 not in held}

    def pieces_of(streams):
        pieces, first = [], 0
        for held in streams:
            pieces += [((k, first), held[k]) for k in range(line)]
            first += held[0].shape[0]
        return pieces

    places = jnp.stack([at_place(place, k) if paired else (place - k) % line for k in range(line)])
    places = places.astype(jnp.int32)

    owners = [(t, s) for t in range(tok_count) for s in range(sides)]
    groups = [[t * feat_count + p * sides + s for t, s in owners] for p in range(line)]
    listed = block_pairs.reshape(tok_count, line, sides * pairs, 2)
    listed = lax.dynamic_index_in_dim(listed, place, 1, keepdims=False).reshape(len(owners), pairs, 2)
    stream = (side - listed // own_blocks % sides) % sides
    slots = listed // (own_blocks * sides) * (own_blocks * sides) + stream * own_blocks + listed % own_blocks
    away = jnp.stack([
        (tok + d // sides) % tok_count * sides + (side + d) % sides for d in range(len(owners))
    ])
    right_slots = jnp.take(slots[:, :, 1], away, axis=0).reshape(-1)
    sources = jnp.stack([
        (tok - d // sides) % tok_count * sides + (side - d) % sides for d in range(len(owners))
    ]).astype(jnp.int32)

    def to_owners(tiles):
        return lax.all_to_all(
            tiles, ("tok", "feat"), split_axis=0, concat_axis=0, axis_index_groups=groups, tiled=True
        )

    def to_owner(tiles, d):
        if d == 0:
            return tiles
        perm = []
        for t, s in owners:
            to_t, to_s = (t + d // sides) % tok_count, (s + d) % sides
            perm += [
                (t * feat_count + p * sides + s, to_t * feat_count + p * sides + to_s) for p in range(line)
            ]
        return lax.ppermute(tiles, ("tok", "feat"), perm)

    own_in = blocks_of(span_input, side)
    span_input, own_in = after(span_input, own_in)
    others_in, others_out = from_sides(span_input), from_sides(span_output)
    own_out = blocks_of(span_output, side)
    streams_in = [far_hops(own_in)]
    if sides > 1:
        others_in, streams_in[0][1] = after(others_in, streams_in[0][1])
        streams_in += [far_hops(other) for other in others_in]
    streams_in[0].update(last_hops(streams_in[0]))
    unit = jnp.concatenate([own_out] + others_out, 0)
    units = [unit[:, c * chunk : (c + 1) * chunk] for c in range(chunks)]
    units, streams_in[-1] = after(units, streams_in[-1])
    for held in streams_in[1:]:
        held.update(last_hops(held))
    chunks_out = [far_hops(unit) for unit in units]
    pieces = pieces_of(streams_in)
    picked = select_early(places, slots.reshape(-1), pieces, len(owners), False)
    (picked,) = select_late(places, slots.reshape(-1), pieces, picked)
    tiles_in = to_owners(picked).reshape(len(owners), pairs, 2, part, BLK)
    for held in chunks_out:
        held.update(last_hops(held))

    gram_shape = jax.ShapeDtypeStruct((pairs, BLK, BLK), jnp.float32)
    left_shape = jax.ShapeDtypeStruct((pairs, BLK, len(owners) * chunk), span_input.dtype)
    lefts = pairs_call(
        functools.partial(left_kernel, chunks), sources, [], tiles_in, 0, [left_shape] * chunks, "left_tiles"
    )
    pieces = [pieces_of([held]) for held in chunks_out]
    early = [select_early(places, right_slots, p, len(owners), True) for p in pieces]
    early[0], early[-1] = after(early[0], early[-1])
    cross = []
    for c in range(chunks):
        final = c + 1 == chunks
        picked = select_late(places, right_slots, pieces[c], early[c])
        if final:
            picked, lefts = after(picked, lefts)
        got = [to_owner(tiles, d) for d, tiles in enumerate(picked)]
        if final:
            (gram,) = pairs_call(
                functools.partial(gram_kernel, inverse, chunks), sources, lefts, tiles_in, 1,
                [gram_shape], "gram_sum",
            )
            cross, gram = after(list(cross), gram)
        cross = sum_call(
            functools.partial(cross_kernel, inverse, len(got)), [lefts[c]] + got + list(cross),
            [gram_shape], "cross_sum",
        )
    (cross,) = cross
    return gram, cross


def solution(mesh):
    return jax.shard_map(
        body,
        mesh=mesh,
        in_specs=(P("tok", "feat"), P("tok", "feat"), P()),
        out_specs=(P(("tok", "feat"), None, None), P(("tok", "feat"), None, None)),
        check_vma=False,
    )
```

```python
import functools

import jax
import jax.numpy as jnp
from jax import lax
from jax.experimental import pallas as pl
from jax.experimental.pallas import tpu as pltpu
from jax.sharding import PartitionSpec as P

BLK = 128
SELECT_LIMIT = 56 << 20
SUM_LIMIT = 20 << 20


def select_kernel(where, groups, outs, late, places_ref, table_ref, *refs):
    arrays = len(where)
    pieces, out_refs, rest = refs[:arrays], refs[arrays : arrays + outs], refs[arrays + outs :]
    list_ref, held, stage, sems, out_sems = rest
    per = held.shape[0] // places_ref.shape[0]
    copies = [
        pltpu.make_async_copy(
            piece, held.at[pl.ds(places_ref[k] * per + first, piece.shape[0])], sems.at[n]
        )
        for n, (piece, (k, first)) in enumerate(zip(pieces, where))
    ]
    for copy in copies:
        copy.start()
    k, first, blocks = late
    begin = places_ref[k] * per + first

    def note(i, found):
        slot = table_ref[i] - begin
        list_ref[found + 1] = i
        return found + jnp.logical_and(slot >= 0, slot < blocks).astype(jnp.int32)

    list_ref[0] = lax.fori_loop(0, table_ref.shape[0], note, 0, unroll=4)
    for copy in copies:
        copy.wait()
    count = stage.shape[0] // groups
    copies = []
    for g in range(groups):

        @pl.loop(0, count, unroll=4)
        def _(i, g=g):
            stage[g * count + i] = held[table_ref[g * count + i]]

        part = pl.ds(g * count, count)
        out = out_refs[g] if outs > 1 else out_refs[0].at[part]
        copies.append(pltpu.make_async_copy(stage.at[part], out, out_sems.at[g]))
        copies[-1].start()
    for copy in copies:
        copy.wait()


def late_kernel(k, first, per, outs, places_ref, table_ref, list_ref, piece, *refs):
    out_refs, out_sem = refs[outs:-1], refs[-1]
    begin = places_ref[k] * per + first
    count = out_refs[0].shape[0]
    found = list_ref[0]

    @pl.loop(0, found)
    def _(n):
        i = list_ref[n + 1]
        source = piece.at[table_ref[i] - begin]
        if outs == 1:
            pltpu.make_async_copy(source, out_refs[0].at[i], out_sem).start()
        for g in range(outs if outs > 1 else 0):

            @pl.when(i // count == g)
            def _(g=g):
                pltpu.make_async_copy(source, out_refs[g].at[i % count], out_sem).start()

    @pl.loop(0, found)
    def _(n):
        pltpu.make_async_copy(piece.at[0], out_refs[0].at[0], out_sem).wait()


def select_early(places, table, pieces, groups, apart):
    total = sum(array.shape[0] for _, array in pieces)
    (k, first), last = pieces[-1]
    where, arrays = [w for w, _ in pieces[:-1]], [array for _, array in pieces[:-1]]
    blocks, rows, blk = last.shape
    count = table.shape[0]
    outs = groups if apart else 1
    picked = pl.pallas_call(
        functools.partial(select_kernel, where, groups, outs, (k, first, blocks)),
        out_shape=[jax.ShapeDtypeStruct((count // outs, rows, blk), last.dtype)] * outs
        + [jax.ShapeDtypeStruct((count + 2,), jnp.int32)],
        in_specs=[pl.BlockSpec(memory_space=pltpu.SMEM)] * 2
        + [pl.BlockSpec(memory_space=pl.ANY)] * len(arrays),
        out_specs=[pl.BlockSpec(memory_space=pl.ANY)] * outs + [pl.BlockSpec(memory_space=pltpu.SMEM)],
        scratch_shapes=[
            pltpu.VMEM((total, rows, blk), last.dtype),
            pltpu.VMEM((count, rows, blk), last.dtype),
            pltpu.SemaphoreType.DMA((len(arrays),)),
            pltpu.SemaphoreType.DMA((groups,)),
        ],
        compiler_params=pltpu.CompilerParams(vmem_limit_bytes=SELECT_LIMIT),
        name="select_tiles",
    )(places, table, *arrays)
    return list(picked)


def select_late(places, table, pieces, picked):
    *picked, listed = picked
    (k, first), piece = pieces[-1]
    outs = len(picked)
    per = sum(array.shape[0] for _, array in pieces) // places.shape[0]
    return pl.pallas_call(
        functools.partial(late_kernel, k, first, per, outs),
        out_shape=[jax.ShapeDtypeStruct(p.shape, p.dtype) for p in picked],
        in_specs=[pl.BlockSpec(memory_space=pltpu.SMEM)] * 3
        + [pl.BlockSpec(memory_space=pltpu.VMEM)]
        + [pl.BlockSpec(memory_space=pl.ANY)] * outs,
        out_specs=[pl.BlockSpec(memory_space=pl.ANY)] * outs,
        scratch_shapes=[pltpu.SemaphoreType.DMA],
        input_output_aliases={4 + i: i for i in range(outs)},
        compiler_params=pltpu.CompilerParams(vmem_limit_bytes=SELECT_LIMIT),
        name="late_tiles",
    )(places, table, listed, piece, *picked)


def rows_in_order(order_ref, tiles, p, rows):
    return jnp.concatenate(
        [tiles[order_ref[d], p, 0, rows] for d in range(order_ref.shape[0])], 0
    )


def left_kernel(chunks, order_ref, tiles, *left_refs):
    chunk = tiles.shape[3] // chunks
    for p in range(tiles.shape[1]):
        for c, left_ref in enumerate(left_refs):
            left_ref[p] = rows_in_order(order_ref, tiles, p, slice(c * chunk, (c + 1) * chunk)).T


def gram_kernel(inverse, chunks, order_ref, *refs):
    lefts, (tiles, out_ref) = refs[:chunks], refs[chunks:]
    chunk = tiles.shape[3] // chunks
    for p in range(tiles.shape[1]):
        total = jnp.zeros(out_ref.shape[1:], jnp.float32)
        for c, left_ref in enumerate(lefts):
            right = rows_in_order(order_ref, tiles, p, slice(c * chunk, (c + 1) * chunk))
            total += jnp.dot(left_ref[p], right, preferred_element_type=jnp.float32)
        out_ref[p] = total * inverse


def pairs_call(kernel, order, lefts, tiles, which, outs, name):
    groups, pairs, _, rows, blk = tiles.shape
    step = pairs // 2 if pairs % 2 == 0 else pairs

    def some(array):
        return pl.BlockSpec((step,) + array.shape[1:], lambda p: (p, 0, 0))

    return pl.pallas_call(
        kernel,
        grid=(pairs // step,),
        out_shape=outs,
        in_specs=[pl.BlockSpec(memory_space=pltpu.SMEM)]
        + [some(left) for left in lefts]
        + [pl.BlockSpec((groups, step, 1, rows, blk), lambda p: (0, p, which, 0, 0))],
        out_specs=[some(out) for out in outs],
        compiler_params=pltpu.CompilerParams(vmem_limit_bytes=SUM_LIMIT),
        name=name,
    )(order, *lefts, tiles)


def cross_kernel(inverse, parts, left_ref, *refs):
    tiles, before, out_ref = refs[:parts], refs[parts:-1], refs[-1]
    pairs = out_ref.shape[0]

    @pl.loop(0, pairs, unroll=4)
    def _(p):
        right = jnp.concatenate([ref[p] for ref in tiles], 0)
        total = jnp.dot(left_ref[p], right, preferred_element_type=jnp.float32) * inverse
        out_ref[p] = total + before[0][p] if before else total


def sum_call(kernel, operands, outs, name):
    return pl.pallas_call(
        kernel,
        out_shape=outs,
        in_specs=[
            pl.BlockSpec(memory_space=pltpu.SMEM if operand.ndim == 1 else pltpu.VMEM)
            for operand in operands
        ],
        out_specs=[pl.BlockSpec(memory_space=pltpu.VMEM)] * len(outs),
        compiler_params=pltpu.CompilerParams(vmem_limit_bytes=SUM_LIMIT),
        name=name,
    )(*operands)


def after(values, done):
    return lax.optimization_barrier((values, done))


def body(span_input, span_output, block_pairs):
    tok_count = lax.axis_size("tok")
    feat_count = lax.axis_size("feat")
    tok = lax.axis_index("tok")
    feat = lax.axis_index("feat")
    rows, width = span_input.shape
    inverse = 1.0 / (tok_count * rows)
    pairs = block_pairs.shape[0] // (tok_count * feat_count)
    own_blocks = width // BLK
    sides = 2 if feat_count % 2 == 0 and rows % 32 == 0 else 1
    line = feat_count // sides
    place, side = feat // sides, feat % sides
    part = rows // sides
    chunks = 2 if part % 32 == 0 else 1
    chunk = part // chunks
    paired = line & (line - 1) == 0

    def blocks_of(array, which):
        taken = lax.dynamic_slice_in_dim(array, which * part, part, 0)
        return taken.reshape(part, own_blocks, BLK).transpose(1, 0, 2)

    def from_sides(array):
        return [
            lax.ppermute(
                blocks_of(array, (side + d) % sides), "feat",
                [(f, f // sides * sides + (f % sides + d) % sides) for f in range(feat_count)],
            )
            for d in range(1, sides)
        ]

    def at_place(p, k):
        return p ^ k if paired else (p + k) % line

    def hop(piece, k):
        return lax.ppermute(piece, "feat", [
            (f, at_place(f // sides, k) * sides + f % sides) for f in range(feat_count)
        ])

    def far_hops(unit):
        held = {0: unit}
        if not paired:
            held.update({k: hop(unit, k) for k in range(1, line)})
            return held
        k = line // 2
        while k > 1:
            held.update({m ^ k: hop(piece, k) for m, piece in list(held.items())})
            k //= 2
        if line > 1:
            held[1] = hop(unit, 1)
        return held

    def last_hops(held):
        return {m ^ 1: hop(held[m], 1) for m in held if m > 1 and m ^ 1 not in held}

    def pieces_of(streams):
        pieces, first = [], 0
        for held in streams:
            pieces += [((k, first), held[k]) for k in range(line)]
            first += held[0].shape[0]
        return pieces

    places = jnp.stack([at_place(place, k) if paired else (place - k) % line for k in range(line)])
    places = places.astype(jnp.int32)

    owners = [(t, s) for t in range(tok_count) for s in range(sides)]
    groups = [[t * feat_count + p * sides + s for t, s in owners] for p in range(line)]
    listed = block_pairs.reshape(tok_count, line, sides * pairs, 2)
    listed = lax.dynamic_index_in_dim(listed, place, 1, keepdims=False).reshape(len(owners), pairs, 2)
    stream = (side - listed // own_blocks % sides) % sides
    slots = listed // (own_blocks * sides) * (own_blocks * sides) + stream * own_blocks + listed % own_blocks
    away = jnp.stack([
        (tok + d // sides) % tok_count * sides + (side + d) % sides for d in range(len(owners))
    ])
    right_slots = jnp.take(slots[:, :, 1], away, axis=0).reshape(-1)
    sources = jnp.stack([
        (tok - d // sides) % tok_count * sides + (side - d) % sides for d in range(len(owners))
    ]).astype(jnp.int32)

    def to_owners(tiles):
        return lax.all_to_all(
            tiles, ("tok", "feat"), split_axis=0, concat_axis=0, axis_index_groups=groups, tiled=True
        )

    def to_owner(tiles, d):
        if d == 0:
            return tiles
        perm = []
        for t, s in owners:
            to_t, to_s = (t + d // sides) % tok_count, (s + d) % sides
            perm += [
                (t * feat_count + p * sides + s, to_t * feat_count + p * sides + to_s) for p in range(line)
            ]
        return lax.ppermute(tiles, ("tok", "feat"), perm)

    own_in = blocks_of(span_input, side)
    span_input, own_in = after(span_input, own_in)
    others_in, others_out = from_sides(span_input), from_sides(span_output)
    own_out = blocks_of(span_output, side)
    streams_in = [far_hops(own_in)]
    if sides > 1:
        others_in, streams_in[0][1] = after(others_in, streams_in[0][1])
        streams_in += [far_hops(other) for other in others_in]
    streams_in[0].update(last_hops(streams_in[0]))
    unit = jnp.concatenate([own_out] + others_out, 0)
    units = [unit[:, c * chunk : (c + 1) * chunk] for c in range(chunks)]
    units, streams_in[-1] = after(units, streams_in[-1])
    for held in streams_in[1:]:
        held.update(last_hops(held))
    chunks_out = [far_hops(unit) for unit in units]
    pieces = pieces_of(streams_in)
    picked = select_early(places, slots.reshape(-1), pieces, len(owners), False)
    (picked,) = select_late(places, slots.reshape(-1), pieces, picked)
    tiles_in = to_owners(picked).reshape(len(owners), pairs, 2, part, BLK)
    for held in chunks_out:
        held.update(last_hops(held))

    gram_shape = jax.ShapeDtypeStruct((pairs, BLK, BLK), jnp.float32)
    left_shape = jax.ShapeDtypeStruct((pairs, BLK, len(owners) * chunk), span_input.dtype)
    lefts = pairs_call(
        functools.partial(left_kernel, chunks), sources, [], tiles_in, 0, [left_shape] * chunks, "left_tiles"
    )
    pieces = [pieces_of([held]) for held in chunks_out]
    early = [select_early(places, right_slots, p, len(owners), True) for p in pieces]
    early[0], early[-1] = after(early[0], early[-1])
    cross = []
    for c in range(chunks):
        final = c + 1 == chunks
        picked = select_late(places, right_slots, pieces[c], early[c])
        if final:
            picked, lefts = after(picked, lefts)
        got = [to_owner(tiles, d) for d, tiles in enumerate(picked)]
        if final:
            (gram,) = pairs_call(
                functools.partial(gram_kernel, inverse, chunks), sources, lefts, tiles_in, 1,
                [gram_shape], "gram_sum",
            )
            cross, gram = after(list(cross), gram)
        cross = sum_call(
            functools.partial(cross_kernel, inverse, len(got)), [lefts[c]] + got + list(cross),
            [gram_shape], "cross_sum",
        )
    (cross,) = cross
    return gram, cross


def solution(mesh):
    return jax.shard_map(
        body,
        mesh=mesh,
        in_specs=(P("tok", "feat"), P("tok", "feat"), P()),
        out_specs=(P(("tok", "feat"), None, None), P(("tok", "feat"), None, None)),
        check_vma=False,
    )
```

```python
import functools

import jax
import jax.numpy as jnp
from jax import lax
from jax.experimental import pallas as pl
from jax.experimental.pallas import tpu as pltpu
from jax.sharding import PartitionSpec as P

BLK = 128
SELECT_LIMIT = 56 << 20
SUM_LIMIT = 20 << 20


def select_kernel(where, groups, outs, late, places_ref, table_ref, *refs):
    arrays = len(where)
    pieces, out_refs, rest = refs[:arrays], refs[arrays : arrays + outs], refs[arrays + outs :]
    list_ref, held, stage, sems, out_sems = rest
    per = held.shape[0] // places_ref.shape[0]
    copies = [
        pltpu.make_async_copy(
            piece, held.at[pl.ds(places_ref[k] * per + first, piece.shape[0])], sems.at[n]
        )
        for n, (piece, (k, first)) in enumerate(zip(pieces, where))
    ]
    for copy in copies:
        copy.start()
    k, first, blocks = late
    begin = places_ref[k] * per + first

    def note(i, found):
        slot = table_ref[i] - begin
        list_ref[found + 1] = i
        return found + jnp.logical_and(slot >= 0, slot < blocks).astype(jnp.int32)

    list_ref[0] = lax.fori_loop(0, table_ref.shape[0], note, 0, unroll=4)
    for copy in copies:
        copy.wait()
    count = stage.shape[0] // groups
    copies = []
    for g in range(groups):

        @pl.loop(0, count, unroll=4)
        def _(i, g=g):
            stage[g * count + i] = held[table_ref[g * count + i]]

        part = pl.ds(g * count, count)
        out = out_refs[g] if outs > 1 else out_refs[0].at[part]
        copies.append(pltpu.make_async_copy(stage.at[part], out, out_sems.at[g]))
        copies[-1].start()
    for copy in copies:
        copy.wait()


def late_kernel(k, first, per, outs, places_ref, table_ref, list_ref, piece, *refs):
    out_refs, out_sem = refs[outs:-1], refs[-1]
    begin = places_ref[k] * per + first
    count = out_refs[0].shape[0]
    found = list_ref[0]

    @pl.loop(0, found)
    def _(n):
        i = list_ref[n + 1]
        source = piece.at[table_ref[i] - begin]
        if outs == 1:
            pltpu.make_async_copy(source, out_refs[0].at[i], out_sem).start()
        for g in range(outs if outs > 1 else 0):

            @pl.when(i // count == g)
            def _(g=g):
                pltpu.make_async_copy(source, out_refs[g].at[i % count], out_sem).start()

    @pl.loop(0, found)
    def _(n):
        pltpu.make_async_copy(piece.at[0], out_refs[0].at[0], out_sem).wait()


def select_early(places, table, pieces, groups, apart):
    total = sum(array.shape[0] for _, array in pieces)
    (k, first), last = pieces[-1]
    where, arrays = [w for w, _ in pieces[:-1]], [array for _, array in pieces[:-1]]
    blocks, rows, blk = last.shape
    count = table.shape[0]
    outs = groups if apart else 1
    picked = pl.pallas_call(
        functools.partial(select_kernel, where, groups, outs, (k, first, blocks)),
        out_shape=[jax.ShapeDtypeStruct((count // outs, rows, blk), last.dtype)] * outs
        + [jax.ShapeDtypeStruct((count + 2,), jnp.int32)],
        in_specs=[pl.BlockSpec(memory_space=pltpu.SMEM)] * 2
        + [pl.BlockSpec(memory_space=pl.ANY)] * len(arrays),
        out_specs=[pl.BlockSpec(memory_space=pl.ANY)] * outs + [pl.BlockSpec(memory_space=pltpu.SMEM)],
        scratch_shapes=[
            pltpu.VMEM((total, rows, blk), last.dtype),
            pltpu.VMEM((count, rows, blk), last.dtype),
            pltpu.SemaphoreType.DMA((len(arrays),)),
            pltpu.SemaphoreType.DMA((groups,)),
        ],
        compiler_params=pltpu.CompilerParams(vmem_limit_bytes=SELECT_LIMIT),
        name="select_tiles",
    )(places, table, *arrays)
    return list(picked)


def select_late(places, table, pieces, picked):
    *picked, listed = picked
    (k, first), piece = pieces[-1]
    outs = len(picked)
    per = sum(array.shape[0] for _, array in pieces) // places.shape[0]
    return pl.pallas_call(
        functools.partial(late_kernel, k, first, per, outs),
        out_shape=[jax.ShapeDtypeStruct(p.shape, p.dtype) for p in picked],
        in_specs=[pl.BlockSpec(memory_space=pltpu.SMEM)] * 3
        + [pl.BlockSpec(memory_space=pltpu.VMEM)]
        + [pl.BlockSpec(memory_space=pl.ANY)] * outs,
        out_specs=[pl.BlockSpec(memory_space=pl.ANY)] * outs,
        scratch_shapes=[pltpu.SemaphoreType.DMA],
        input_output_aliases={4 + i: i for i in range(outs)},
        compiler_params=pltpu.CompilerParams(vmem_limit_bytes=SELECT_LIMIT),
        name="late_tiles",
    )(places, table, listed, piece, *picked)


def rows_in_order(order_ref, tiles, p, rows):
    return jnp.concatenate(
        [tiles[order_ref[d], p, 0, rows] for d in range(order_ref.shape[0])], 0
    )


def left_kernel(chunks, order_ref, tiles, *left_refs):
    chunk = tiles.shape[3] // chunks
    for p in range(tiles.shape[1]):
        for c, left_ref in enumerate(left_refs):
            left_ref[p] = rows_in_order(order_ref, tiles, p, slice(c * chunk, (c + 1) * chunk)).T


def gram_kernel(inverse, chunks, order_ref, *refs):
    lefts, (tiles, out_ref) = refs[:chunks], refs[chunks:]
    chunk = tiles.shape[3] // chunks
    for p in range(tiles.shape[1]):
        total = jnp.zeros(out_ref.shape[1:], jnp.float32)
        for c, left_ref in enumerate(lefts):
            right = rows_in_order(order_ref, tiles, p, slice(c * chunk, (c + 1) * chunk))
            total += jnp.dot(left_ref[p], right, preferred_element_type=jnp.float32)
        out_ref[p] = total * inverse


def pairs_call(kernel, order, lefts, tiles, which, outs, name):
    groups, pairs, _, rows, blk = tiles.shape
    step = pairs // 2 if pairs % 2 == 0 else pairs

    def some(array):
        return pl.BlockSpec((step,) + array.shape[1:], lambda p: (p, 0, 0))

    return pl.pallas_call(
        kernel,
        grid=(pairs // step,),
        out_shape=outs,
        in_specs=[pl.BlockSpec(memory_space=pltpu.SMEM)]
        + [some(left) for left in lefts]
        + [pl.BlockSpec((groups, step, 1, rows, blk), lambda p: (0, p, which, 0, 0))],
        out_specs=[some(out) for out in outs],
        compiler_params=pltpu.CompilerParams(vmem_limit_bytes=SUM_LIMIT),
        name=name,
    )(order, *lefts, tiles)


def cross_kernel(inverse, parts, left_ref, *refs):
    tiles, before, out_ref = refs[:parts], refs[parts:-1], refs[-1]
    pairs = out_ref.shape[0]

    @pl.loop(0, pairs, unroll=4)
    def _(p):
        right = jnp.concatenate([ref[p] for ref in tiles], 0)
        total = jnp.dot(left_ref[p], right, preferred_element_type=jnp.float32) * inverse
        out_ref[p] = total + before[0][p] if before else total


def sum_call(kernel, operands, outs, name):
    return pl.pallas_call(
        kernel,
        out_shape=outs,
        in_specs=[
            pl.BlockSpec(memory_space=pltpu.SMEM if operand.ndim == 1 else pltpu.VMEM)
            for operand in operands
        ],
        out_specs=[pl.BlockSpec(memory_space=pltpu.VMEM)] * len(outs),
        compiler_params=pltpu.CompilerParams(vmem_limit_bytes=SUM_LIMIT),
        name=name,
    )(*operands)


def after(values, done):
    return lax.optimization_barrier((values, done))


def body(span_input, span_output, block_pairs):
    tok_count = lax.axis_size("tok")
    feat_count = lax.axis_size("feat")
    tok = lax.axis_index("tok")
    feat = lax.axis_index("feat")
    rows, width = span_input.shape
    inverse = 1.0 / (tok_count * rows)
    pairs = block_pairs.shape[0] // (tok_count * feat_count)
    own_blocks = width // BLK
    sides = 2 if feat_count % 2 == 0 and rows % 32 == 0 else 1
    line = feat_count // sides
    place, side = feat // sides, feat % sides
    part = rows // sides
    chunks = 2 if part % 32 == 0 else 1
    chunk = part // chunks
    paired = line & (line - 1) == 0

    def blocks_of(array, which):
        taken = lax.dynamic_slice_in_dim(array, which * part, part, 0)
        return taken.reshape(part, own_blocks, BLK).transpose(1, 0, 2)

    def from_sides(array):
        return [
            lax.ppermute(
                blocks_of(array, (side + d) % sides), "feat",
                [(f, f // sides * sides + (f % sides + d) % sides) for f in range(feat_count)],
            )
            for d in range(1, sides)
        ]

    def at_place(p, k):
        return p ^ k if paired else (p + k) % line

    def hop(piece, k):
        return lax.ppermute(piece, "feat", [
            (f, at_place(f // sides, k) * sides + f % sides) for f in range(feat_count)
        ])

    def far_hops(unit):
        held = {0: unit}
        if not paired:
            held.update({k: hop(unit, k) for k in range(1, line)})
            return held
        k = line // 2
        while k > 1:
            held.update({m ^ k: hop(piece, k) for m, piece in list(held.items())})
            k //= 2
        if line > 1:
            held[1] = hop(unit, 1)
        return held

    def last_hops(held):
        return {m ^ 1: hop(held[m], 1) for m in held if m > 1 and m ^ 1 not in held}

    def pieces_of(streams):
        pieces, first = [], 0
        for held in streams:
            pieces += [((k, first), held[k]) for k in range(line)]
            first += held[0].shape[0]
        return pieces

    places = jnp.stack([at_place(place, k) if paired else (place - k) % line for k in range(line)])
    places = places.astype(jnp.int32)

    owners = [(t, s) for t in range(tok_count) for s in range(sides)]
    groups = [[t * feat_count + p * sides + s for t, s in owners] for p in range(line)]
    listed = block_pairs.reshape(tok_count, line, sides * pairs, 2)
    listed = lax.dynamic_index_in_dim(listed, place, 1, keepdims=False).reshape(len(owners), pairs, 2)
    stream = (side - listed // own_blocks % sides) % sides
    slots = listed // (own_blocks * sides) * (own_blocks * sides) + stream * own_blocks + listed % own_blocks
    away = jnp.stack([
        (tok + d // sides) % tok_count * sides + (side + d) % sides for d in range(len(owners))
    ])
    right_slots = jnp.take(slots[:, :, 1], away, axis=0).reshape(-1)
    sources = jnp.stack([
        (tok - d // sides) % tok_count * sides + (side - d) % sides for d in range(len(owners))
    ]).astype(jnp.int32)

    def to_owners(tiles):
        return lax.all_to_all(
            tiles, ("tok", "feat"), split_axis=0, concat_axis=0, axis_index_groups=groups, tiled=True
        )

    def to_owner(tiles, d):
        if d == 0:
            return tiles
        perm = []
        for t, s in owners:
            to_t, to_s = (t + d // sides) % tok_count, (s + d) % sides
            perm += [
                (t * feat_count + p * sides + s, to_t * feat_count + p * sides + to_s) for p in range(line)
            ]
        return lax.ppermute(tiles, ("tok", "feat"), perm)

    own_in = blocks_of(span_input, side)
    span_input, own_in = after(span_input, own_in)
    others_in, others_out = from_sides(span_input), from_sides(span_output)
    own_out = blocks_of(span_output, side)
    streams_in = [far_hops(own_in)]
    if sides > 1:
        others_in, streams_in[0][1] = after(others_in, streams_in[0][1])
        streams_in += [far_hops(other) for other in others_in]
    streams_in[0].update(last_hops(streams_in[0]))
    unit = jnp.concatenate([own_out] + others_out, 0)
    units = [unit[:, c * chunk : (c + 1) * chunk] for c in range(chunks)]
    units, streams_in[-1] = after(units, streams_in[-1])
    for held in streams_in[1:]:
        held.update(last_hops(held))
    chunks_out = [far_hops(unit) for unit in units]
    pieces = pieces_of(streams_in)
    picked = select_early(places, slots.reshape(-1), pieces, len(owners), False)
    (picked,) = select_late(places, slots.reshape(-1), pieces, picked)
    tiles_in = to_owners(picked).reshape(len(owners), pairs, 2, part, BLK)
    for held in chunks_out:
        held.update(last_hops(held))

    gram_shape = jax.ShapeDtypeStruct((pairs, BLK, BLK), jnp.float32)
    left_shape = jax.ShapeDtypeStruct((pairs, BLK, len(owners) * chunk), span_input.dtype)
    lefts = pairs_call(
        functools.partial(left_kernel, chunks), sources, [], tiles_in, 0, [left_shape] * chunks, "left_tiles"
    )
    pieces = [pieces_of([held]) for held in chunks_out]
    early = [select_early(places, right_slots, p, len(owners), True) for p in pieces]
    early[0], early[-1] = after(early[0], early[-1])
    cross = []
    for c in range(chunks):
        final = c + 1 == chunks
        if final:
            early[c], lefts = after(early[c], lefts)
        picked = select_late(places, right_slots, pieces[c], early[c])
        got = [to_owner(tiles, d) for d, tiles in enumerate(picked)]
        if final:
            (gram,) = pairs_call(
                functools.partial(gram_kernel, inverse, chunks), sources, lefts, tiles_in, 1,
                [gram_shape], "gram_sum",
            )
            cross, gram = after(list(cross), gram)
        cross = sum_call(
            functools.partial(cross_kernel, inverse, len(got)), [lefts[c]] + got + list(cross),
            [gram_shape], "cross_sum",
        )
    (cross,) = cross
    return gram, cross


def solution(mesh):
    return jax.shard_map(
        body,
        mesh=mesh,
        in_specs=(P("tok", "feat"), P("tok", "feat"), P()),
        out_specs=(P(("tok", "feat"), None, None), P(("tok", "feat"), None, None)),
        check_vma=False,
    )
```
